512 devices in a mesh: samp: 128 (over z, x, core), rep: 4 (over y).
Axes of the slice: x: 4, y: 4, z: 16, core: 2. Of those that a mesh axis runs over, the one named last changes fastest.
Arguments:
- read_blocks: bfloat16 [4, 512, 221, 8, 128], P('rep', 'samp'), may hold values from -6 to 6
- block_counts: int32 [4, 128], P('rep'), may hold values from 1 to 4, as said below
- block_reads: int32 [4, 512], P('rep'), may hold values from 32 to 128
- block_starts: int32 [4, 512], P('rep'), may hold values from 0 to 803
- conv_weight: bfloat16 [3, 8, 64], replicated, may hold values from -1.25 to 1.25
- conv_bias: float32 [64], replicated, may hold values from -3 to 3
- mix_weight: bfloat16 [64, 64], replicated, may hold values from -0.75 to 0.75
- pool_query: float32 [64], replicated, may hold values from -0.75 to 0.75
- site_cotangent: float32 [4, 128, 64, 1024], P('rep', 'samp'), may hold values from -2.5 to 2.5
Outputs:
- pooled_sites: float32 [4, 128, 64, 1024], P('rep', 'samp')
- grad_conv: float32 [3, 8, 64], replicated
- grad_bias: float32 [64], replicated
- grad_mix: float32 [64, 64], replicated
- grad_query: float32 [64], replicated
The draws below stay inside these ranges and needn't reach their ends.
Inputs may be any that keep to these rules, and one draw needn't show every extreme that they name: `block_counts`: samples 2k and 2k + 1 of a window form a tumor and normal pair: one of them holds 2 to 4 blocks, the other 1 or 2, and the pair holds at most 6 blocks; in every window the first and the last pair hold 4 and 2 blocks; in the last pair the sample of even index holds the 4 in windows of even index, the sample of odd index in windows of odd index.
All inputs are finite; a program needn't handle non-finite values.
Results may differ from the reference program's by a relative error of at most 0.0034.
Values may be sent and summed in bfloat16 or wider, within the bound.
No kernel may reach another device: no remote copies, remote signals or barrier semaphores. Data moves between devices by JAX's collectives and lax.ppermute only.
A program may use at most 128 MiB of HBM per device.

```python
import jax
import jax.numpy as jnp
from jax import lax

P_SIZE = 221
C = 8
R = 128
F = 64
OWN = 4
CAP = 3
SITES = 1024
WINDOWS = 4
SAMPLES = 128


def draw_block_counts(key, part):
    key = jax.random.fold_in(key, 7)
    first_key, second_key, third_key = jax.random.split(key, 3)
    half = SAMPLES // 2
    tumor = jax.random.randint(first_key, (WINDOWS, half), 2, OWN + 1)
    tumor = tumor.at[:, 0].set(OWN).at[:, half - 1].set(OWN)
    normal = jax.random.randint(second_key, (WINDOWS, half), 1, 3)
    normal = normal.at[:, 0].set(2).at[:, half - 1].set(2)
    normal = jnp.minimum(normal, 2 * CAP - tumor)
    placing = jax.random.randint(third_key, (WINDOWS, half), 0, 2)
    window_parity = jnp.arange(WINDOWS, dtype=jnp.int32) % 2
    placing = placing.at[:, half - 1].set(window_parity)
    leading = jnp.where(placing == 0, tumor, normal)
    trailing = jnp.where(placing == 0, normal, tumor)
    return jnp.stack([leading, trailing], axis=2).reshape(WINDOWS, SAMPLES).astype(jnp.int32)


def place_ends(values, own_key, least, top_value):
    extent = values.shape
    place = [jax.random.randint(jax.random.fold_in(own_key, axis), (), 0, extent[axis]) for axis in range(len(extent))]
    values = values.at[tuple(place)].set(least)
    longest = extent.index(max(extent))
    place[longest] = (place[longest] + 1) % extent[longest]
    return values.at[tuple(place)].set(top_value)


def steps_of(rng, extent, cuts, least, high):
    def one(dim, shards_of):
        draws = jax.random.uniform(jax.random.fold_in(jax.random.fold_in(rng, 6), dim), (shards_of,), jnp.float32, least / len(cuts), high / len(cuts))
        return jnp.repeat(jnp.exp(draws), extent[dim] // shards_of).reshape((-1,) + (1,) * (len(extent) - dim - 1))

    level = one(*cuts[0])
    for cut in cuts[1:]:
        level = level * one(*cut)
    return level


def centred(key, dims, deviation, reach, shards=(), held_as=jnp.bfloat16):
    entries = jax.random.normal(key, dims, jnp.float32) * deviation
    if len(shards) > 0:
        entries = steps_of(key, dims, shards, -0.22, 0.18) * entries
    return jnp.clip(entries, min=-reach, max=reach).astype(held_as)


def setup_inputs(seed: int = 0) -> dict:
    key_of = jax.random.split(jax.random.key(seed), 10)
    return {
        "read_blocks": centred(key_of[0], (WINDOWS, SAMPLES * OWN, P_SIZE, C, R), 1.0, 6.0, ((0, 4), (1, 128))),
        "block_counts": draw_block_counts(jax.random.fold_in(key_of[9], 71), 0),
        "block_reads": place_ends(jax.random.randint(key_of[2], (WINDOWS, SAMPLES * OWN), R // 4, R + 1), jax.random.fold_in(key_of[2], 1), R // 4, R).astype(jnp.int32),
        "block_starts": place_ends(jax.random.randint(key_of[3], (WINDOWS, SAMPLES * OWN), 0, SITES - P_SIZE + 1), jax.random.fold_in(key_of[3], 1), 0, SITES - P_SIZE).astype(jnp.int32),
        "conv_weight": centred(key_of[4], (3, C, F), (3 * C) ** -0.5, 1.25),
        "conv_bias": centred(key_of[5], (F,), 0.5, 3.0, (), jnp.float32),
        "mix_weight": centred(key_of[6], (F, F), F ** -0.5, 0.75),
        "pool_query": centred(key_of[7], (F,), F ** -0.5, 0.75, (), jnp.float32),
        "site_cotangent": centred(key_of[8], (WINDOWS, SAMPLES, F, SITES), (4 * (WINDOWS * SAMPLES) ** -0.5), 2.5, ((0, 4), (1, 128)), jnp.float32),
    }


def make_taps(pileup):
    border = jnp.zeros_like(pileup[:1])
    padded = jnp.concatenate([border, pileup, border], axis=0)
    return jnp.stack([padded[:-2], padded[1:-1], padded[2:]], axis=1)


def pooling_terms(second_out, pool_query, live_mask):
    feature = jax.nn.silu(second_out)
    opening = jax.nn.sigmoid(jnp.sum(feature * pool_query[None, :, None], axis=1))
    return feature, opening, opening * live_mask[None, :]


def first_layer(pileup, conv_weight, conv_bias):
    shifted = make_taps(pileup.astype(jnp.float32))
    pre_relu = jnp.einsum("ptcr,tcf->pfr", shifted, conv_weight.astype(jnp.float32), precision=lax.Precision.HIGHEST)
    return jax.nn.relu(pre_relu + conv_bias[None, :, None]).astype(jnp.bfloat16)


def second_layer(hidden, mix_weight):
    return jnp.einsum("pgr,gf->pfr", hidden.astype(jnp.float32), mix_weight.astype(jnp.float32), precision=lax.Precision.HIGHEST)


def forward_slot(pileup, live_mask, conv_weight, conv_bias, mix_weight, pool_query):
    hidden = first_layer(pileup, conv_weight, conv_bias)
    second_out = second_layer(hidden, mix_weight)
    feature, opening, read_weight = pooling_terms(second_out, pool_query, live_mask)
    numerator = jnp.sum(feature * read_weight[:, None, :], axis=2).T
    denominator = jnp.sum(read_weight, axis=1)
    return numerator, denominator, hidden, second_out


def backward_slot(pileup, live_mask, hidden, second_out, mix_weight, pool_query, d_numerator, d_denominator):
    feature, opening, read_weight = pooling_terms(second_out, pool_query, live_mask)
    d_weight = jnp.sum(feature * d_numerator.T[:, :, None], axis=1) + d_denominator[:, None]
    d_score = d_weight * live_mask[None, :] * opening * (1.0 - opening)
    d_feature = d_numerator.T[:, :, None] * read_weight[:, None, :] + d_score[:, None, :] * pool_query[None, :, None]
    g_query = jnp.sum(d_score[:, None, :] * feature, axis=(0, 2))
    sigmoid_out = jax.nn.sigmoid(second_out)
    d_second = (d_feature * sigmoid_out * (1.0 + second_out * (1.0 - sigmoid_out))).astype(jnp.bfloat16)
    g_mix = jnp.einsum("pgr,pfr->gf", hidden.astype(jnp.float32), d_second.astype(jnp.float32), precision=lax.Precision.HIGHEST)
    d_hidden = jnp.einsum("pfr,gf->pgr", d_second.astype(jnp.float32), mix_weight.astype(jnp.float32), precision=lax.Precision.HIGHEST)
    d_relu = jnp.where(hidden > 0, d_hidden, 0.0).astype(jnp.bfloat16)
    g_bias = jnp.sum(d_relu.astype(jnp.float32), axis=(0, 2))
    g_conv = jnp.einsum("ptcr,pfr->tcf", make_taps(pileup.astype(jnp.float32)), d_relu.astype(jnp.float32), precision=lax.Precision.HIGHEST)
    return g_conv, g_bias, g_mix, g_query


def place_window(numerator, denominator, start, site_total):
    anchor = jnp.zeros_like(start)
    num_win = lax.dynamic_update_slice(jnp.zeros((numerator.shape[0], site_total), jnp.float32), numerator, (anchor, start))
    den_win = lax.dynamic_update_slice(jnp.zeros((site_total,), jnp.float32), denominator, (start,))
    return num_win, den_win


def cut_window(num_win, den_win, start, width):
    anchor = jnp.zeros_like(start)
    return (lax.dynamic_slice(num_win, (anchor, start), (num_win.shape[0], width)),
            lax.dynamic_slice(den_win, (start,), (width,)))


def owner_step(site_num, site_den, cotangent):
    safe_den = jnp.maximum(site_den, 1.0)
    pooled = site_num / safe_den
    d_num = cotangent / safe_den
    d_den = jnp.where(site_den > 1.0, -jnp.sum(cotangent * site_num, axis=0) / (safe_den * safe_den), 0.0)
    return pooled, d_num, d_den


def reference(read_blocks, block_counts, block_reads, block_starts, conv_weight, conv_bias, mix_weight, pool_query, site_cotangent):
    owners = WINDOWS * SAMPLES
    flat_blocks = read_blocks.reshape(owners, OWN, P_SIZE, C, R)
    flat_counts = block_counts.reshape(owners)
    flat_reads = block_reads.reshape(owners, OWN)
    flat_starts = block_starts.reshape(owners, OWN)
    flat_cotangent = site_cotangent.reshape(owners, F, SITES)
    read_index = jnp.arange(R, dtype=jnp.int32)
    slot_index = jnp.arange(OWN, dtype=jnp.int32)

    def owner_work(element):
        pileups, count, reads, starts, cotangent = element

        def forward_step(running, slot):
            pileup, read_count, start, index = slot
            live_mask = ((read_index < read_count) & (index < count)).astype(jnp.float32)

            def active(block_in):
                outcome = forward_slot(block_in, live_mask, conv_weight, conv_bias, mix_weight, pool_query)
                return place_window(outcome[0], outcome[1], start, SITES)

            def resting(block_in):
                return jnp.zeros((F, SITES), jnp.float32), jnp.zeros((SITES,), jnp.float32)

            num_win, den_win = lax.cond(index < count, active, resting, pileup)
            return (running[0] + num_win, running[1] + den_win), None

        start_sums = (jnp.zeros((F, SITES), jnp.float32), jnp.zeros((SITES,), jnp.float32))
        (site_num, site_den), _ = lax.scan(forward_step, start_sums, (pileups, reads, starts, slot_index))
        pooled, d_num, d_den = owner_step(site_num, site_den, cotangent)

        def backward_step(running, slot):
            pileup, read_count, start, index = slot
            live_mask = ((read_index < read_count) & (index < count)).astype(jnp.float32)

            def active(block_in):
                outcome = forward_slot(block_in, live_mask, conv_weight, conv_bias, mix_weight, pool_query)
                d_numerator, d_denominator = cut_window(d_num, d_den, start, P_SIZE)
                return backward_slot(block_in, live_mask, outcome[2], outcome[3], mix_weight, pool_query, d_numerator, d_denominator)

            def resting(block_in):
                return (jnp.zeros((3, C, F), jnp.float32), jnp.zeros((F,), jnp.float32),
                        jnp.zeros((F, F), jnp.float32), jnp.zeros((F,), jnp.float32))

            terms = lax.cond(index < count, active, resting, pileup)
            return tuple(accumulated + increment for accumulated, increment in zip(running, terms)), None

        start_grads = (jnp.zeros((3, C, F), jnp.float32), jnp.zeros((F,), jnp.float32),
                       jnp.zeros((F, F), jnp.float32), jnp.zeros((F,), jnp.float32))
        gradients, _ = lax.scan(backward_step, start_grads, (pileups, reads, starts, slot_index))
        return pooled, gradients

    pooled, gradients = lax.map(owner_work, (flat_blocks, flat_counts, flat_reads, flat_starts, flat_cotangent))
    return (pooled.reshape(WINDOWS, SAMPLES, F, SITES), jnp.sum(gradients[0], axis=0), jnp.sum(gradients[1], axis=0),
            jnp.sum(gradients[2], axis=0), jnp.sum(gradients[3], axis=0))
```

```python
import jax
import jax.numpy as jnp
from jax import lax
from jax.experimental import pallas as pl
from jax.experimental.pallas import tpu as pltpu
from jax.sharding import PartitionSpec as P

POS = 221
CH = 8
R = 128
F = 64
OWN = 4
SITES = 1024
HALF = 112
GROUP = 8
CHUNKS = HALF // GROUP
XPOS = 2 * HALF + 2
WIN = SITES + 8
SPARE = OWN * CHUNKS

F32 = jnp.float32
BF = jnp.bfloat16
NT = (((1,), (1,)), ((), ()))


def mm(a, b):
    return jnp.dot(a, b, preferred_element_type=F32)


def mm_nt(a, b):
    return lax.dot_general(a, b, NT, preferred_element_type=F32)


def split2(v):
    hi = v.astype(BF)
    return hi, (v - hi.astype(F32)).astype(BF)


def halves(v):
    zero = jnp.zeros((8, R), v.dtype)
    left = jnp.concatenate([v[:, :R], zero], axis=1)
    right = jnp.concatenate([zero, v[:, R:]], axis=1)
    return jnp.concatenate([left, right], axis=0)


def pooling_kernel(
    dev, counts, reads, starts, x, conv_w, bias, mix, query, cot,
    pooled, grads,
    hid, feat, slope, weight_rows, gate_rows, score_rows, second_ring, relu_ring,
    w_num, w_den, d_num, d_den, acc_mix, acc_conv, acc_query,
):
    me = dev[0]
    count = counts[0, me]
    total = count * CHUNKS

    zeros = lambda *s: jnp.zeros(s, F32)
    cw = conv_w[...].astype(F32)
    b = bias[...]
    b_hi = b.astype(BF).astype(F32)
    b_mid = (b - b_hi).astype(BF).astype(F32)
    b_lo = b - b_hi - b_mid
    b_rows = jnp.concatenate([b_hi, b_mid, b_lo, zeros(13, F)], axis=0)
    even = jnp.concatenate([cw, zeros(8, F), b_rows, zeros(80, F)], axis=0)
    odd = jnp.concatenate([zeros(8, F), cw, b_rows, zeros(80, F)], axis=0)
    conv_lhs = jnp.concatenate([even.T, odd.T], axis=0)[:, :48].astype(BF)
    mix_f = mix[...].astype(F32)
    pad_mix = jnp.concatenate([mix_f, zeros(64, F)], axis=0)
    mix_t = (0.5 * pad_mix.T[:, :F]).astype(BF)
    mix_b = mix[...]
    q = 0.5 * query[...]
    q_hi = q.astype(BF).astype(F32)
    q_lo = q - q_hi
    q_hi8 = jnp.broadcast_to(q_hi, (8, F))
    q_lo8 = jnp.broadcast_to(q_lo, (8, F))
    query_lhs = jnp.concatenate([q_hi8, q_lo8], axis=0).astype(BF)
    ones = jnp.ones((16, 2 * R), BF)
    row8 = lax.broadcasted_iota(jnp.int32, (8, 2 * R), 0)
    lane8 = lax.broadcasted_iota(jnp.int32, (8, 2 * R), 1)
    row16 = lax.broadcasted_iota(jnp.int32, (16, F), 0)
    lane_mod = lax.broadcasted_iota(jnp.int32, (F, 128), 1) % GROUP

    def place(k):
        slot = jnp.minimum(k // CHUNKS, OWN - 1)
        return slot, k - (k // CHUNKS) * CHUNKS

    def window(slot, c, i):
        base = pl.multiple_of(c * (GROUP * CH), 16)
        left = x[slot, pl.ds(base + 16 * i, 32), :]
        right = x[slot, pl.ds(base + HALF * CH + 16 * i, 32), :]
        return jnp.concatenate(
            [jnp.concatenate([left, right], axis=1), ones], axis=0
        )

    w_num[...] = jnp.zeros(w_num.shape, F32)
    w_den[...] = jnp.zeros(w_den.shape, F32)

    def first_stage(k):
        slot, c = place(k)
        for i in range(GROUP // 2):
            pre = mm(conv_lhs, window(slot, c, i))
            hid[k, 128 * i : 128 * i + 128, :] = jnp.maximum(pre, 0.0).astype(BF)

    def second_stage(k):
        for j in range(GROUP):
            rows = slice(F * j, F * j + F)
            h = mm(mix_t, hid[k, rows, :])
            t = jnp.tanh(h)
            u = h * t
            feat[k, rows, :] = (h + u).astype(BF)
            slope[k, rows, :] = ((1.0 + t) * (1.0 + (h - u))).astype(BF)

    def score_stage(k):
        slot, c = place(k)
        score = jnp.zeros((8, 2 * R), F32)
        for j in range(GROUP):
            s = mm(query_lhs, feat[k, F * j : F * j + F, :])
            score = jnp.where(row8 == j, s[:8] + s[8:], score)
        opening = 0.5 + 0.5 * jnp.tanh(score)
        read = jnp.where(lane8 < R, lane8, lane8 - R)
        position = jnp.where(lane8 < R, row8, row8 + HALF) + GROUP * c
        live = (read < reads[0, me * OWN + slot]) & (position < POS)
        weight = jnp.where(live, opening, 0.0)
        weight_rows[k] = weight
        gate_rows[k] = weight * (1.0 - opening)

    def pool_stage(k, valid):
        slot, c = place(k)
        weight = weight_rows[k]
        lhs = halves(weight).astype(BF)
        num = jnp.zeros((16, F), F32)
        for j in range(GROUP):
            n = mm_nt(lhs, feat[k, F * j : F * j + F, :])
            num = jnp.where((row16 % GROUP) == j, n, num)
        den_l = jnp.sum(weight[:, :R], axis=1, keepdims=True)
        den_r = jnp.sum(weight[:, R:], axis=1, keepdims=True)
        first = starts[0, me * OWN + slot] + GROUP * c
        for part, den, at in ((num[:8], den_l, first), (num[8:], den_r, first + HALF)):
            here = pl.ds(at, 8)
            w_num[here, :] += jnp.where(valid, part, 0.0)
            w_den[here, :] += jnp.where(valid, jnp.broadcast_to(den, (8, 128)), 0.0)

    @pl.loop(0, total + 3)
    def _(i):
        pool_stage(jnp.maximum(i - 3, 0), i >= 3)
        score_stage(jnp.clip(i - 2, 0, SPARE))
        second_stage(jnp.clip(i - 1, 0, SPARE))
        first_stage(jnp.minimum(i, SPARE))

    d_num[SITES:, :] = jnp.zeros((WIN - SITES, 128), F32)
    d_den[SITES:, :] = jnp.zeros((WIN - SITES, 128), F32)

    @pl.loop(0, SITES // 128)
    def _(i):
        at = pl.multiple_of(i * 128, 128)
        here = pl.ds(at, 128)
        num = w_num[here, :]
        den = w_den[here, :]
        safe = jnp.maximum(den, 1.0)
        inv = 1.0 / safe
        inv_f = inv[:, :F]
        out = jnp.concatenate([num * inv_f, jnp.zeros((128, F), F32)], axis=1)
        pooled[:, here] = out.T[:F]
        cot_t = jnp.concatenate([cot[:, here], jnp.zeros((F, 128), F32)], axis=0).T
        dn = cot_t * inv
        d_num[here, :] = dn
        inner = jnp.sum(dn[:, :F] * num, axis=1, keepdims=True)
        d_den[here, :] = jnp.where(den > 1.0, -(jnp.broadcast_to(inner, (128, 128)) * inv), 0.0)

    acc_mix[...] = jnp.zeros(acc_mix.shape, F32)
    acc_conv[...] = jnp.zeros(acc_conv.shape, F32)
    acc_query[...] = jnp.zeros(acc_query.shape, F32)

    def cut(k):
        slot, c = place(k)
        first = starts[0, me * OWN + slot] + GROUP * c
        return first, jnp.concatenate(
            [d_num[pl.ds(first, 8), :], d_num[pl.ds(first + HALF, 8), :]], axis=0
        )

    def weight_stage(k):
        first, dn = cut(k)
        hi, lo = split2(dn[:, :F])
        lhs = jnp.concatenate([hi, lo], axis=0)
        d_weight = jnp.zeros((8, 2 * R), F32)
        for j in range(GROUP):
            w = mm(lhs, feat[k, F * j : F * j + F, :])
            w = w[:16] + w[16:]
            w = jnp.concatenate([w[:8, :R], w[8:, R:]], axis=1)
            d_weight = jnp.where(row8 == j, w, d_weight)
        dd = jnp.concatenate([d_den[pl.ds(first, 8), :], d_den[pl.ds(first + HALF, 8), :]], axis=1)
        score_rows[k % 4] = (d_weight + dd) * gate_rows[k]

    def second_back(k):
        _, dn = cut(k)
        half = 0.5 * dn
        hi = half.astype(BF).astype(F32)
        lo = half - hi
        pad_q = lambda v: jnp.concatenate([jnp.broadcast_to(v, (16, F)), zeros(16, F)], axis=1)
        lhs_t = jnp.concatenate(
            [hi, hi, lo, pad_q(q_hi), pad_q(q_hi), pad_q(q_lo), zeros(32, 128)], axis=0
        )
        lhs = lhs_t.T[:F]
        w_hi, w_lo = split2(weight_rows[k])
        s_hi, s_lo = split2(score_rows[k % 4])
        w_hi, w_lo, s_hi, s_lo = halves_bf(w_hi), halves_bf(w_lo), halves_bf(s_hi), halves_bf(s_lo)
        rhs = jnp.concatenate([w_hi, w_lo, w_hi, s_hi, s_lo, s_hi], axis=0)
        for j in range(GROUP):
            rows = slice(F * j, F * j + F)
            part = jnp.where(lane_mod == j, lhs, 0.0).astype(BF)[:, :96]
            d_feat = mm(part, rhs)
            second_ring[k % 2, rows, :] = (d_feat * slope[k, rows, :].astype(F32)).astype(BF)

    def halves_bf(v):
        return halves(v.astype(F32)).astype(BF)

    def relu_back(k, valid):
        lhs, rhs = [], []
        for j in range(GROUP):
            rows = slice(F * j, F * j + F)
            d2 = second_ring[k % 2, rows, :]
            h = hid[k, rows, :]
            lhs.append(h)
            rhs.append(d2)
            dh = mm(mix_b, d2).astype(BF)
            relu_ring[k % 2, rows, :] = jnp.where(h > 0, dh, jnp.zeros_like(dh))
        g = mm_nt(jnp.concatenate(lhs, axis=1), jnp.concatenate(rhs, axis=1))
        acc_mix[...] += jnp.where(valid, g, 0.0)

    def weights_back(k, valid):
        slot, c = place(k)
        wins = [window(slot, c, i) for i in range(GROUP // 2)]
        lhs = jnp.concatenate(
            [relu_ring[k % 2, 128 * i : 128 * i + 128, :] for i in range(GROUP // 2)], axis=1
        )
        g = mm_nt(lhs, jnp.concatenate(wins, axis=1))
        acc_conv[...] += jnp.where(valid, g, 0.0)
        ds = halves(score_rows[k % 4])
        row = lax.broadcasted_iota(jnp.int32, (16, 2 * R), 0) % GROUP
        lhs, rhs = [], []
        for j in range(GROUP):
            hi, lo = split2(jnp.where(row == j, ds, 0.0))
            lhs.append(jnp.concatenate([hi, lo], axis=0))
            rhs.append(feat[k, F * j : F * j + F, :])
        g = mm_nt(jnp.concatenate(lhs, axis=1), jnp.concatenate(rhs, axis=1))
        acc_query[...] += jnp.where(valid, g, 0.0)

    @pl.loop(0, total + 3)
    def _(i):
        weights_back(jnp.maximum(i - 3, 0), i >= 3)
        relu_back(jnp.clip(i - 2, 0, SPARE - 1), (i >= 2) & (i < total + 2))
        second_back(jnp.clip(i - 1, 0, SPARE - 1))
        weight_stage(jnp.minimum(i, SPARE - 1))

    turned = jnp.concatenate([acc_conv[...], zeros(128, 80)], axis=1).T
    g_conv = turned[0:24, :F] + turned[8:32, F:]
    g_bias = turned[32:33, :F] + turned[32:33, F:]
    g_query = jnp.sum(acc_query[...], axis=0, keepdims=True)
    rest = jnp.concatenate([g_conv, g_bias, g_query, zeros(6, F)], axis=0)
    gm = acc_mix[...]
    grads[0:32, :] = jnp.concatenate([gm[:32], gm[32:]], axis=1)
    grads[32:48, :] = jnp.concatenate([rest[:16], rest[16:]], axis=1)


def run_kernel(dev, counts, reads, starts, x, conv_w, bias, mix, query, cot, interpret=False):
    smem = pl.BlockSpec(memory_space=pltpu.SMEM)
    vmem = pl.BlockSpec(memory_space=pltpu.VMEM)
    big = (SPARE + 1, GROUP * F, 2 * R)
    return pl.pallas_call(
        pooling_kernel,
        out_shape=(
            jax.ShapeDtypeStruct((F, SITES), F32),
            jax.ShapeDtypeStruct((48, 128), F32),
        ),
        in_specs=[smem] * 4 + [vmem] * 6,
        out_specs=(vmem, vmem),
        scratch_shapes=[
            pltpu.VMEM(big, BF),
            pltpu.VMEM(big, BF),
            pltpu.VMEM(big, BF),
            pltpu.VMEM((SPARE + 1, 8, 2 * R), F32),
            pltpu.VMEM((SPARE + 1, 8, 2 * R), F32),
            pltpu.VMEM((4, 8, 2 * R), F32),
            pltpu.VMEM((2, GROUP * F, 2 * R), BF),
            pltpu.VMEM((2, GROUP * F, 2 * R), BF),
            pltpu.VMEM((WIN, F), F32),
            pltpu.VMEM((WIN, 128), F32),
            pltpu.VMEM((WIN, 128), F32),
            pltpu.VMEM((WIN, 128), F32),
            pltpu.VMEM((F, F), F32),
            pltpu.VMEM((128, 48), F32),
            pltpu.VMEM((32, F), F32),
        ],
        compiler_params=pltpu.CompilerParams(vmem_limit_bytes=60 * 2**20),
        interpret=interpret,
    )(dev, counts, reads, starts, x, conv_w, bias, mix, query, cot)


def pad_blocks(blocks):
    padded = jnp.pad(blocks, ((0, 0), (1, XPOS - POS - 1), (0, 0), (0, 0)))
    return padded.reshape(OWN, XPOS * CH, R)


def on_device(
    read_blocks, block_counts, block_reads, block_starts,
    conv_weight, conv_bias, mix_weight, pool_query, site_cotangent,
):
    dev = lax.axis_index("samp").astype(jnp.int32).reshape(1)
    pooled, grads = run_kernel(
        dev, block_counts, block_reads, block_starts,
        pad_blocks(read_blocks[0]),
        conv_weight.reshape(3 * CH, F), conv_bias.reshape(1, F), mix_weight,
        pool_query.reshape(1, F), site_cotangent[0, 0],
    )
    for bit in range(7):
        stride = 1 << bit
        grads = grads + lax.ppermute(grads, "samp", [(i, i ^ stride) for i in range(128)])
    for bit in range(2):
        stride = 1 << bit
        grads = grads + lax.ppermute(grads, "rep", [(i, i ^ stride) for i in range(4)])
    g_mix = jnp.concatenate([grads[:32, :F], grads[:32, F:]], axis=0)
    rest = jnp.concatenate([grads[32:, :F], grads[32:, F:]], axis=0)
    return (pooled[None, None], rest[:24].reshape(3, CH, F), rest[24], g_mix, rest[25])


def solution(mesh):
    in_specs = (
        P("rep", "samp", None, None, None),
        P("rep", None),
        P("rep", None),
        P("rep", None),
        P(),
        P(),
        P(),
        P(),
        P("rep", "samp", None, None),
    )
    out_specs = (P("rep", "samp", None, None), P(), P(), P(), P())
    return jax.shard_map(
        on_device, mesh=mesh, in_specs=in_specs, out_specs=out_specs, check_vma=False
    )
```

```python
import jax
import jax.numpy as jnp
from jax import lax
from jax.experimental import pallas as pl
from jax.experimental.pallas import tpu as pltpu
from jax.sharding import PartitionSpec as P

POS = 221
CH = 8
R = 128
F = 64
OWN = 4
SITES = 1024
HALF = 112
GROUP = 8
CHUNKS = HALF // GROUP
XPOS = 2 * HALF + 2
WIN = SITES + 8
SPARE = OWN * CHUNKS

SAMP = ("z_high", "z_low", "x", "core")

F32 = jnp.float32
BF = jnp.bfloat16
NT = (((1,), (1,)), ((), ()))


def mm(a, b):
    return jnp.dot(a, b, preferred_element_type=F32)


def mm_nt(a, b):
    return lax.dot_general(a, b, NT, preferred_element_type=F32)


def split2(v):
    hi = v.astype(BF)
    return hi, (v - hi.astype(F32)).astype(BF)


def halves(v):
    zero = jnp.zeros((8, R), v.dtype)
    left = jnp.concatenate([v[:, :R], zero], axis=1)
    right = jnp.concatenate([zero, v[:, R:]], axis=1)
    return jnp.concatenate([left, right], axis=0)


def pooling_kernel(
    dev, counts, reads, starts, x_hbm, conv_w, bias, mix, query, cot,
    pooled, grads,
    x, hid, feat, slope, weight_rows, gate_rows, query_rows,
    hid_0, hid_1, feat_0, feat_1, score_0, score_1, second_0, second_1, relu_0, relu_1,
    w_num, w_den, d_num, d_den, acc_mix, acc_conv, acc_query, sems,
):
    me = dev[0]
    count = counts[0, me]
    total = count * CHUNKS
    hid_ring = (hid_0, hid_1)
    feat_ring, score_ring = (feat_0, feat_1), (score_0, score_1)
    second_ring, relu_ring = (second_0, second_1), (relu_0, relu_1)

    copies = [
        pltpu.make_async_copy(x_hbm.at[0, s], x.at[s, pl.ds(1, POS)], sems.at[s])
        for s in range(OWN)
    ]
    for copy in copies:
        copy.start()
    for s in range(OWN):
        x[s, 0] = jnp.zeros((CH, R), BF)
        x[s, POS + 1 :] = jnp.zeros((XPOS - POS - 1, CH, R), BF)

    zeros = lambda *s: jnp.zeros(s, F32)
    cw = conv_w[...].astype(F32)
    b = bias[...]
    b_hi = b.astype(BF).astype(F32)
    b_mid = (b - b_hi).astype(BF).astype(F32)
    b_lo = b - b_hi - b_mid
    b_rows = jnp.concatenate([b_hi, b_mid, b_lo, zeros(13, F)], axis=0)
    even = jnp.concatenate([cw, zeros(8, F), b_rows, zeros(80, F)], axis=0)
    odd = jnp.concatenate([zeros(8, F), cw, b_rows, zeros(80, F)], axis=0)
    conv_lhs = jnp.concatenate([even.T, odd.T], axis=0)[:, :48].astype(BF)
    pad_mix = jnp.concatenate([mix[...].astype(F32), zeros(64, F)], axis=0)
    mix_t = (0.5 * pad_mix.T[:, :F]).astype(BF)
    mix_b = mix[...]
    q = 0.5 * query[...]
    q_hi = q.astype(BF).astype(F32)
    q_lo = q - q_hi
    query_lhs = jnp.concatenate(
        [jnp.broadcast_to(q_hi, (8, F)), jnp.broadcast_to(q_lo, (8, F))], axis=0
    ).astype(BF)
    query_rows[...] = jnp.concatenate([jnp.broadcast_to(q, (128, F)), zeros(128, F)], axis=1).T[:F]
    ones = jnp.ones((16, 2 * R), BF)
    row8 = lax.broadcasted_iota(jnp.int32, (8, 2 * R), 0)
    lane8 = lax.broadcasted_iota(jnp.int32, (8, 2 * R), 1)
    row16 = lax.broadcasted_iota(jnp.int32, (16, F), 0) % GROUP

    def place(k):
        slot = jnp.int32(0)
        for s in range(1, OWN):
            slot = slot + (k >= s * CHUNKS).astype(jnp.int32)
        return slot, k - slot * CHUNKS

    def window(slot, c, i):
        at = c * GROUP + 2 * i
        left = x[slot, pl.ds(at, 4)].reshape(32, R)
        right = x[slot, pl.ds(at + HALF, 4)].reshape(32, R)
        return jnp.concatenate([jnp.concatenate([left, right], axis=1), ones], axis=0)

    w_num[...] = jnp.zeros(w_num.shape, F32)
    w_den[...] = jnp.zeros(w_den.shape, F32)
    for copy in copies:
        copy.wait()

    def first_dots(k, half, i):
        slot, c = place(jnp.minimum(k, SPARE - 1))
        pre = mm(conv_lhs, window(slot, c, i)).astype(BF)
        rows = slice(128 * i, 128 * i + 128)
        relu = jnp.maximum(pre, jnp.zeros_like(pre))
        hid[k, rows, :] = relu
        hid_ring[half][rows, :] = relu

    def second_dots(half):
        return [mm(mix_t, hid_ring[half][F * j : F * j + F, :]) for j in range(GROUP)]

    def second_rest(k, dots):
        for j, h in enumerate(dots):
            rows = slice(F * j, F * j + F)
            a = 1.0 + jnp.tanh(h)
            f = h * a
            feat[k, rows, :] = f.astype(BF)
            slope[k, rows, :] = (a * (1.0 + ((h + h) - f))).astype(BF)

    def score_stage(k, half):
        slot, c = place(k)
        score = jnp.zeros((8, 2 * R), F32)
        for j in range(GROUP):
            s = mm(query_lhs, feat_ring[half][F * j : F * j + F, :])
            score = jnp.where(row8 == j, s[:8] + s[8:], score)
        opening = 0.5 + 0.5 * jnp.tanh(score)
        read = jnp.where(lane8 < R, lane8, lane8 - R)
        position = jnp.where(lane8 < R, row8, row8 + HALF) + GROUP * c
        live = (read < reads[0, me * OWN + slot]) & (position < POS)
        weight = jnp.where(live, opening, 0.0)
        weight_rows[k] = weight
        gate_rows[k] = weight * (1.0 - opening)
        return weight

    def pool_dot(half, lhs, num, j):
        n = mm_nt(lhs, feat_ring[half][F * j : F * j + F, :])
        return jnp.where(row16 == j, n, num)

    def pool_rest(k, weight, num, valid):
        slot, c = place(k)
        den_l = jnp.sum(weight[:, :R], axis=1, keepdims=True)
        den_r = jnp.sum(weight[:, R:], axis=1, keepdims=True)
        first = starts[0, me * OWN + slot] + GROUP * c
        for part, den, at in ((num[:8], den_l, first), (num[8:], den_r, first + HALF)):
            here = pl.ds(at, 8)
            w_num[here, :] += jnp.where(valid, part, 0.0)
            w_den[here, :] += jnp.where(valid, jnp.broadcast_to(den, (8, 128)), 0.0)

    @pl.loop(0, total // 2 + 2)
    def _(i):
        new = [jnp.minimum(2 * i + half, SPARE) for half in range(2)]
        mid = [jnp.clip(2 * i + half - 2, 0, SPARE) for half in range(2)]
        old = [jnp.maximum(2 * i + half - 4, 0) for half in range(2)]
        dots_0 = second_dots(0)
        weights = [score_stage(old[half], half) for half in range(2)]
        dots_1 = second_dots(1)
        second_rest(mid[0], dots_0)
        for n in range(GROUP // 2):
            first_dots(new[0], 0, n)
        second_rest(mid[1], dots_1)
        lhs = [halves(w).astype(BF) for w in weights]
        nums = [jnp.zeros((16, F), F32)] * 2
        for n in range(GROUP // 2):
            first_dots(new[1], 1, n)
            for half in range(2):
                for j in (2 * n, 2 * n + 1):
                    nums[half] = pool_dot(half, lhs[half], nums[half], j)
        for half in range(2):
            pool_rest(old[half], weights[half], nums[half], i >= 2)
            feat_ring[half][...] = feat[mid[half]]

    d_num[SITES:, :] = jnp.zeros((WIN - SITES, 128), F32)
    d_den[SITES:, :] = jnp.zeros((WIN - SITES, 128), F32)
    for i in range(SITES // 128):
        here = slice(128 * i, 128 * i + 128)
        num = w_num[here, :]
        den = w_den[here, :]
        inv = 1.0 / jnp.maximum(den, 1.0)
        out = jnp.concatenate([num * inv[:, :F], jnp.zeros((128, F), F32)], axis=1)
        pooled[:, here] = out.T[:F]
        cot_t = jnp.concatenate([cot[:, here], jnp.zeros((F, 128), F32)], axis=0).T
        dn = cot_t * inv
        d_num[here, :] = dn
        inner = jnp.sum(dn[:, :F] * num, axis=1, keepdims=True)
        d_den[here, :] = jnp.where(den > 1.0, -(jnp.broadcast_to(inner, (128, 128)) * inv), 0.0)

    acc_mix[...] = jnp.zeros(acc_mix.shape, F32)
    acc_conv[...] = jnp.zeros(acc_conv.shape, F32)
    acc_query[...] = jnp.zeros(acc_query.shape, F32)

    def cut(k):
        slot, c = place(k)
        first = starts[0, me * OWN + slot] + GROUP * c
        return first, jnp.concatenate(
            [d_num[pl.ds(first, 8), :], d_num[pl.ds(first + HALF, 8), :]], axis=0
        )

    def weight_dot(lhs, k, d_weight, j):
        w = mm(lhs, feat[k, F * j : F * j + F, :])
        w = jnp.concatenate([w[:8, :R] + w[16:24, :R], w[8:16, R:] + w[24:, R:]], axis=1)
        return jnp.where(row8 == j, w, d_weight)

    def second_back(k, half, valid):
        _, dn = cut(k)
        turned = jnp.concatenate([0.5 * dn, zeros(112, 128)], axis=0).T[:F]
        q = query_rows[...]
        sums = zeros(F, R)
        for j in range(GROUP):
            rows = slice(F * j, F * j + F)
            f = feat[k, rows, :].astype(F32)
            e = slope[k, rows, :].astype(F32)
            out = []
            for side in range(2):
                lanes = slice(R * side, R * side + R)
                at = GROUP * side + j
                w = weight_rows[k, j : j + 1, lanes]
                s = score_ring[half][j : j + 1, lanes]
                d_feat = turned[:, at : at + 1] * w + q * s
                out.append((d_feat * e[:, lanes]).astype(BF))
                sums = sums + f[:, lanes] * s
            second_ring[half][rows, :] = jnp.concatenate(out, axis=1)
        acc_query[...] += jnp.where(valid, sums, 0.0)

    @pl.loop(0, total // 2 + 3)
    def _(i):
        inside = lambda v: (v >= 0) & (v < total)
        bound = lambda v: jnp.clip(v, 0, SPARE - 1)
        for half in range(2):
            k0, k1, k2, k3 = (2 * i + half - 2 * lag for lag in range(4))
            new, old, last = bound(k0), bound(k2), bound(k3)
            slot, c = place(last)
            first, dn = cut(new)
            hi, lo = split2(dn[:, :F])
            lhs = jnp.concatenate([hi, lo], axis=0)
            d_weight = jnp.zeros((8, 2 * R), F32)
            g_conv = zeros(48, 128)
            g_mix = zeros(F, F)
            for n in range(GROUP // 2):
                both = slice(128 * n, 128 * n + 128)
                g_conv += mm_nt(window(slot, c, n), relu_ring[half][both, :])
                h = [hid[old, F * j : F * j + F, :] for j in (2 * n, 2 * n + 1)]
                d2 = [second_ring[half][F * j : F * j + F, :] for j in (2 * n, 2 * n + 1)]
                for j in range(2):
                    dh = mm(mix_b, d2[j]).astype(BF)
                    at = F * (2 * n + j)
                    relu_ring[half][at : at + F, :] = jnp.where(h[j] > 0, dh, jnp.zeros_like(dh))
                g_mix += mm_nt(jnp.concatenate(h, axis=1), jnp.concatenate(d2, axis=1))
                for j in (2 * n, 2 * n + 1):
                    d_weight = weight_dot(lhs, new, d_weight, j)
            second_back(bound(k1), half, inside(k1))
            acc_conv[...] += jnp.where(inside(k3), g_conv, 0.0)
            acc_mix[...] += jnp.where(inside(k2), g_mix, 0.0)
            dd = jnp.concatenate(
                [d_den[pl.ds(first, 8), :], d_den[pl.ds(first + HALF, 8), :]], axis=1
            )
            score_ring[half][...] = (d_weight + dd) * gate_rows[new]

    turned = acc_conv[...]
    g_conv = turned[0:24, :F] + turned[8:32, F:]
    g_bias = turned[32:33, :F] + turned[32:33, F:]
    ones_f = jnp.concatenate([acc_query[...], zeros(F, R)], axis=0).T
    g_query = jnp.sum(ones_f, axis=0, keepdims=True)[:, :F]
    rest = jnp.concatenate([g_conv, g_bias, g_query, zeros(6, F)], axis=0)
    gm = acc_mix[...]
    grads[0:32, :] = jnp.concatenate([gm[:32], gm[32:]], axis=1)
    grads[32:48, :] = jnp.concatenate([rest[:16], rest[16:]], axis=1)


def run_kernel(dev, counts, reads, starts, x, conv_w, bias, mix, query, cot, interpret=False):
    smem = pl.BlockSpec(memory_space=pltpu.SMEM)
    vmem = pl.BlockSpec(memory_space=pltpu.VMEM)
    big = (SPARE + 1, GROUP * F, 2 * R)
    return pl.pallas_call(
        pooling_kernel,
        out_shape=(
            jax.ShapeDtypeStruct((F, SITES), F32),
            jax.ShapeDtypeStruct((48, 128), F32),
        ),
        in_specs=[smem] * 4 + [pl.BlockSpec(memory_space=pl.ANY)] + [vmem] * 5,
        out_specs=(vmem, vmem),
        scratch_shapes=[
            pltpu.VMEM((OWN, XPOS, CH, R), BF),
            pltpu.VMEM(big, BF),
            pltpu.VMEM(big, BF),
            pltpu.VMEM(big, BF),
            pltpu.VMEM((SPARE + 1, 8, 2 * R), F32),
            pltpu.VMEM((SPARE + 1, 8, 2 * R), F32),
            pltpu.VMEM((F, R), F32),
            pltpu.VMEM(big[1:], BF),
            pltpu.VMEM(big[1:], BF),
            pltpu.VMEM(big[1:], BF),
            pltpu.VMEM(big[1:], BF),
            pltpu.VMEM((8, 2 * R), F32),
            pltpu.VMEM((8, 2 * R), F32),
            pltpu.VMEM(big[1:], BF),
            pltpu.VMEM(big[1:], BF),
            pltpu.VMEM(big[1:], BF),
            pltpu.VMEM(big[1:], BF),
            pltpu.VMEM((WIN, F), F32),
            pltpu.VMEM((WIN, 128), F32),
            pltpu.VMEM((WIN, 128), F32),
            pltpu.VMEM((WIN, 128), F32),
            pltpu.VMEM((F, F), F32),
            pltpu.VMEM((48, 128), F32),
            pltpu.VMEM((F, R), F32),
            pltpu.SemaphoreType.DMA((OWN,)),
        ],
        compiler_params=pltpu.CompilerParams(vmem_limit_bytes=60 * 2**20),
        interpret=interpret,
    )(dev, counts, reads, starts, x, conv_w, bias, mix, query, cot)


def on_device(
    read_blocks, block_counts, block_reads, block_starts,
    conv_weight, conv_bias, mix_weight, pool_query, site_cotangent,
):
    dev = lax.axis_index(SAMP).astype(jnp.int32).reshape(1)
    pooled, grads = run_kernel(
        dev, block_counts, block_reads, block_starts,
        read_blocks,
        conv_weight.reshape(3 * CH, F), conv_bias.reshape(1, F), mix_weight,
        pool_query.reshape(1, F), site_cotangent[0, 0],
    )
    for axes, size in ((("x", "core"), 8), (("z_low", "rep"), 8), ("z_high", 8)):
        every = jnp.broadcast_to(grads, (size, *grads.shape))
        grads = jnp.sum(lax.all_to_all(every, axes, 0, 0), axis=0)
    g_mix = jnp.concatenate([grads[:32, :F], grads[:32, F:]], axis=0)
    rest = jnp.concatenate([grads[32:, :F], grads[32:, F:]], axis=0)
    return (pooled[None, None], rest[:24].reshape(3, CH, F), rest[24], g_mix, rest[25])


def solution(mesh):
    split = jax.sharding.Mesh(
        mesh.devices.reshape(8, 2, 4, 2, mesh.shape["rep"]), SAMP + ("rep",)
    )
    in_specs = (
        P("rep", SAMP, None, None, None),
        P("rep", None),
        P("rep", None),
        P("rep", None),
        P(),
        P(),
        P(),
        P(),
        P("rep", SAMP, None, None),
    )
    out_specs = (P("rep", SAMP, None, None), P(), P(), P(), P())
    return jax.shard_map(
        on_device, mesh=split, in_specs=in_specs, out_specs=out_specs, check_vma=False
    )
```

```python
import jax
import jax.numpy as jnp
from jax import lax
from jax.experimental import pallas as pl
from jax.experimental.pallas import tpu as pltpu
from jax.sharding import PartitionSpec as P

POS = 221
CH = 8
R = 128
F = 64
OWN = 4
SITES = 1024
HALF = 112
GROUP = 8
CHUNKS = HALF // GROUP
XPOS = 2 * HALF + 2
WIN = SITES + 8
SPARE = OWN * CHUNKS
STEP = 4

SAMP = ("z_high", "z_low", "x", "core")

F32 = jnp.float32
BF = jnp.bfloat16
NT = (((1,), (1,)), ((), ()))


def mm(a, b):
    return jnp.dot(a, b, preferred_element_type=F32)


def mm_nt(a, b):
    return lax.dot_general(a, b, NT, preferred_element_type=F32)


def split2(v):
    hi = v.astype(BF)
    return hi, (v - hi.astype(F32)).astype(BF)


def spread(v):
    twice = jnp.concatenate([v, v], axis=1)
    row = lax.broadcasted_iota(jnp.int32, twice.shape, 0) % GROUP
    late = lax.broadcasted_iota(jnp.int32, twice.shape, 1) // F
    return jnp.concatenate(
        [jnp.where(row == 2 * m + late, twice, 0.0) for m in range(GROUP // 2)], axis=1
    )


def halves(v):
    zero = jnp.zeros((8, R), v.dtype)
    left = jnp.concatenate([v[:, :R], zero], axis=1)
    right = jnp.concatenate([zero, v[:, R:]], axis=1)
    return jnp.concatenate([left, right], axis=0)


def pooling_kernel(
    dev, counts, reads, starts, x_hbm, conv_w, bias, mix, query, cot,
    pooled, grads,
    x, hid, feat, slope, weight_rows, gate_rows, query_rows,
    w_num, w_den, d_num, d_den, acc_mix, acc_conv, acc_query, sems, *rings,
):
    me = dev[0]
    count = counts[0, me]
    total = count * CHUNKS
    hid_ring, feat_ring, second_ring, relu_ring, score_ring, turned_ring = (
        rings[STEP * n : STEP * n + STEP] for n in range(6)
    )

    copies = [
        pltpu.make_async_copy(x_hbm.at[0, s], x.at[s, pl.ds(1, POS)], sems.at[s])
        for s in range(OWN)
    ]
    for copy in copies:
        copy.start()
    for s in range(OWN):
        x[s, 0] = jnp.zeros((CH, R), BF)
        x[s, POS + 1 :] = jnp.zeros((XPOS - POS - 1, CH, R), BF)

    zeros = lambda *s: jnp.zeros(s, F32)
    cw = conv_w[...].astype(F32)
    b = bias[...]
    b_hi = b.astype(BF).astype(F32)
    b_mid = (b - b_hi).astype(BF).astype(F32)
    b_lo = b - b_hi - b_mid
    b_rows = jnp.concatenate([b_hi, b_mid, b_lo, zeros(13, F)], axis=0)
    even = jnp.concatenate([cw, zeros(8, F), b_rows, zeros(80, F)], axis=0)
    odd = jnp.concatenate([zeros(8, F), cw, b_rows, zeros(80, F)], axis=0)
    conv_lhs = jnp.concatenate([even.T, odd.T], axis=0)[:, :48].astype(BF)
    pad_mix = jnp.concatenate([mix[...].astype(F32), zeros(64, F)], axis=0)
    mix_t = (0.5 * pad_mix.T[:, :F]).astype(BF)
    mix_b = mix[...]
    q = 0.5 * query[...]
    q_hi = q.astype(BF).astype(F32)
    q_lo = q - q_hi
    query_lhs = spread(
        jnp.concatenate([jnp.broadcast_to(q_hi, (8, F)), jnp.broadcast_to(q_lo, (8, F))], axis=0)
    ).astype(BF)
    query_rows[...] = jnp.concatenate([jnp.broadcast_to(q, (128, F)), zeros(128, F)], axis=1).T[:F]
    ones = jnp.ones((16, 2 * R), BF)
    row8 = lax.broadcasted_iota(jnp.int32, (8, 2 * R), 0)
    lane8 = lax.broadcasted_iota(jnp.int32, (8, 2 * R), 1)
    row16 = lax.broadcasted_iota(jnp.int32, (16, 128), 0) % GROUP
    pair16 = row16 // 2

    def place(k):
        slot = jnp.int32(0)
        for s in range(1, OWN):
            slot = slot + (k >= s * CHUNKS).astype(jnp.int32)
        return slot, k - slot * CHUNKS

    def window(slot, c, i):
        at = c * GROUP + 2 * i
        left = x[slot, pl.ds(at, 4)].reshape(32, R)
        right = x[slot, pl.ds(at + HALF, 4)].reshape(32, R)
        return jnp.concatenate([jnp.concatenate([left, right], axis=1), ones], axis=0)

    w_num[...] = jnp.zeros(w_num.shape, F32)
    w_den[...] = jnp.zeros(w_den.shape, F32)
    for copy in copies:
        copy.wait()

    def first_dots(k, half, i):
        slot, c = place(jnp.minimum(k, SPARE - 1))
        pre = mm(conv_lhs, window(slot, c, i)).astype(BF)
        rows = slice(128 * i, 128 * i + 128)
        relu = jnp.maximum(pre, jnp.zeros_like(pre))
        hid[k, rows, :] = relu
        hid_ring[half][rows, :] = relu

    def second_dots(half):
        return [mm(mix_t, hid_ring[half][F * j : F * j + F, :]) for j in range(GROUP)]

    def second_rest(k, dots):
        for j, h in enumerate(dots):
            rows = slice(F * j, F * j + F)
            t = jnp.tanh(h)
            a = 1.0 + t
            f = h * a
            feat[k, rows, :] = f.astype(BF)
            slope[k, rows, :] = (a + f * (1.0 - t)).astype(BF)

    def score_stage(k, half):
        slot, c = place(k)
        score = mm(query_lhs, feat_ring[half][...])
        score = score[:8] + score[8:]
        opening = 0.5 + 0.5 * jnp.tanh(score)
        read = jnp.where(lane8 < R, lane8, lane8 - R)
        position = jnp.where(lane8 < R, row8, row8 + HALF) + GROUP * c
        live = (read < reads[0, me * OWN + slot]) & (position < POS)
        weight = jnp.where(live, opening, 0.0)
        weight_rows[k] = weight
        gate_rows[k] = weight * (1.0 - opening)
        dens = [
            jnp.broadcast_to(jnp.sum(weight[:, at : at + R], axis=1, keepdims=True), (8, 128))
            for at in (0, R)
        ]
        return halves(weight).astype(BF), dens

    def pool_dot(half, lhs, num, n):
        part = mm_nt(lhs, feat_ring[half][256 * n : 256 * n + 256, :])
        for m in range(2):
            num = jnp.where(pair16 == 2 * n + m, part[:, 128 * m : 128 * m + 128], num)
        return num

    def pool_rest(k, dens, num, valid):
        slot, c = place(k)
        first = starts[0, me * OWN + slot] + GROUP * c
        num = jnp.where(row16 % 2 == 0, num, pltpu.roll(num, F, 1))[:, :F]
        for part, den, at in ((num[:8], dens[0], first), (num[8:], dens[1], first + HALF)):
            here = pl.ds(at, 8)
            w_num[here, :] += jnp.where(valid, part, 0.0)
            w_den[here, :] += jnp.where(valid, den, 0.0)

    inside = lambda v: (v >= 0) & (v < total)
    bound = lambda v: jnp.clip(v, 0, SPARE - 1)
    steps = (total + STEP - 1) // STEP

    def forward_step(i, stages):
        first, second, pool = (n in stages for n in range(3))
        chunks = range(STEP)
        new = [jnp.minimum(STEP * i + n, SPARE) for n in chunks]
        mid = [jnp.clip(STEP * (i - 1) + n, 0, SPARE) for n in chunks]
        old = [bound(STEP * (i - 2) + n) for n in chunks]
        nums = [jnp.zeros((16, 128), F32)] * STEP
        dots, weights = {}, {}
        if second:
            dots[0] = second_dots(0)
        if pool:
            weights = {n: score_stage(old[n], n) for n in chunks}
        for n in chunks:
            if second:
                if n + 1 < STEP:
                    dots[n + 1] = second_dots(n + 1)
                second_rest(mid[n], dots.pop(n))
            todo = (2 * n - 2, 2 * n - 1) if pool and n in (1, 2) else ()
            for m in range(GROUP // 2):
                if first:
                    first_dots(new[n], n, m)
                if m % 2:
                    for t in todo:
                        nums[t] = pool_dot(t, weights[t][0], nums[t], m // 2)
            for t in todo:
                pool_rest(old[t], weights[t][1], nums[t], inside(STEP * (i - 2) + t))
        if second:
            for n in chunks:
                feat_ring[n][...] = feat[mid[n]]

    forward_step(0, (0,))
    forward_step(1, (0, 1))

    @pl.loop(2, steps)
    def _(i):
        forward_step(i, (0, 1, 2))

    forward_step(steps, (1, 2))
    forward_step(steps + 1, (2,))

    d_num[SITES:, :] = jnp.zeros((WIN - SITES, 128), F32)
    d_den[SITES:, :] = jnp.zeros((WIN - SITES, 128), F32)
    for i in range(SITES // 128):
        here = slice(128 * i, 128 * i + 128)
        num = w_num[here, :]
        den = w_den[here, :]
        inv = 1.0 / jnp.maximum(den, 1.0)
        out = jnp.concatenate([num * inv[:, :F], jnp.zeros((128, F), F32)], axis=1)
        pooled[:, here] = out.T[:F]
        cot_t = jnp.concatenate([cot[:, here], jnp.zeros((F, 128), F32)], axis=0).T
        dn = cot_t * inv
        d_num[here, :] = dn
        inner = jnp.sum(dn[:, :F] * num, axis=1, keepdims=True)
        d_den[here, :] = jnp.where(den > 1.0, -(jnp.broadcast_to(inner, (128, 128)) * inv), 0.0)

    acc_mix[...] = jnp.zeros(acc_mix.shape, F32)
    acc_conv[...] = jnp.zeros(acc_conv.shape, F32)
    acc_query[...] = jnp.zeros(acc_query.shape, F32)

    def cut(k):
        slot, c = place(k)
        first = starts[0, me * OWN + slot] + GROUP * c
        return first, jnp.concatenate(
            [d_num[pl.ds(first, 8), :], d_num[pl.ds(first + HALF, 8), :]], axis=0
        )

    def second_back(k, half, valid):
        turned = turned_ring[half][...]
        q = query_rows[...]
        sums = zeros(F, R)
        for j in range(GROUP):
            rows = slice(F * j, F * j + F)
            f = feat[k, rows, :].astype(F32)
            e = slope[k, rows, :].astype(F32)
            out = []
            for side in range(2):
                lanes = slice(R * side, R * side + R)
                at = GROUP * side + j
                w = weight_rows[k, j : j + 1, lanes]
                s = score_ring[half][j : j + 1, lanes]
                d_feat = turned[:, at : at + 1] * w + q * s
                out.append((d_feat * e[:, lanes]).astype(BF))
                sums = sums + f[:, lanes] * s
            second_ring[half][rows, :] = jnp.concatenate(out, axis=1)
        acc_query[...] += jnp.where(valid, sums, 0.0)

    def backward_step(i, stages):
        weight, second, relu, conv = (n in stages for n in range(4))
        for half in range(STEP):
            k0, k1, k2, k3 = (STEP * (i - lag) + half for lag in range(4))
            new, old, last = bound(k0), bound(k2), bound(k3)
            slot, c = place(last)
            g_conv = zeros(48, 128)
            g_mix = zeros(F, F)
            for n in range(GROUP // 2):
                both = slice(128 * n, 128 * n + 128)
                if conv:
                    g_conv += mm_nt(window(slot, c, n), relu_ring[half][both, :])
                if relu:
                    h = [hid[old, F * j : F * j + F, :] for j in (2 * n, 2 * n + 1)]
                    d2 = [second_ring[half][F * j : F * j + F, :] for j in (2 * n, 2 * n + 1)]
                    for j in range(2):
                        dh = mm(mix_b, d2[j]).astype(BF)
                        at = F * (2 * n + j)
                        relu_ring[half][at : at + F, :] = jnp.where(
                            h[j] > 0, dh, jnp.zeros_like(dh)
                        )
                    g_mix += mm_nt(jnp.concatenate(h, axis=1), jnp.concatenate(d2, axis=1))
            if second:
                second_back(bound(k1), half, inside(k1))
            if weight:
                first, dn = cut(new)
                hi, lo = split2(spread(dn[:, :F]))
                dw = mm(jnp.concatenate([hi, lo], axis=0), feat[new])
                dw = jnp.concatenate(
                    [dw[:8, :R] + dw[16:24, :R], dw[8:16, R:] + dw[24:, R:]], axis=1
                )
                dd = jnp.concatenate(
                    [d_den[pl.ds(first, 8), :], d_den[pl.ds(first + HALF, 8), :]], axis=1
                )
                score_ring[half][...] = (dw + dd) * gate_rows[new]
                turned_ring[half][...] = jnp.concatenate([0.5 * dn, zeros(112, 128)], axis=0).T[:F]
            if conv:
                acc_conv[...] += jnp.where(inside(k3), g_conv, 0.0)
            if relu:
                acc_mix[...] += jnp.where(inside(k2), g_mix, 0.0)

    backward_step(0, (0,))
    backward_step(1, (0, 1))
    backward_step(2, (0, 1, 2))

    @pl.loop(3, steps)
    def _(i):
        backward_step(i, (0, 1, 2, 3))

    backward_step(steps, (1, 2, 3))
    backward_step(steps + 1, (2, 3))
    backward_step(steps + 2, (3,))

    turned = acc_conv[...]
    g_conv = turned[0:24, :F] + turned[8:32, F:]
    g_bias = turned[32:33, :F] + turned[32:33, F:]
    ones_f = jnp.concatenate([acc_query[...], zeros(F, R)], axis=0).T
    g_query = jnp.sum(ones_f, axis=0, keepdims=True)[:, :F]
    rest = jnp.concatenate([g_conv, g_bias, g_query, zeros(6, F)], axis=0)
    gm = acc_mix[...]
    packed = jnp.concatenate(
        [jnp.concatenate([v[:n], v[n:]], axis=1) for v, n in ((gm, 32), (rest, 16))], axis=0
    )
    for n in range(GROUP):
        grads[n] = packed


def run_kernel(dev, counts, reads, starts, x, conv_w, bias, mix, query, cot, interpret=False):
    smem = pl.BlockSpec(memory_space=pltpu.SMEM)
    vmem = pl.BlockSpec(memory_space=pltpu.VMEM)
    big = (SPARE + 1, GROUP * F, 2 * R)
    return pl.pallas_call(
        pooling_kernel,
        out_shape=(
            jax.ShapeDtypeStruct((F, SITES), F32),
            jax.ShapeDtypeStruct((GROUP, 48, 128), F32),
        ),
        in_specs=[smem] * 4 + [pl.BlockSpec(memory_space=pl.ANY)] + [vmem] * 5,
        out_specs=(vmem, vmem),
        scratch_shapes=[
            pltpu.VMEM((OWN, XPOS, CH, R), BF),
            pltpu.VMEM(big, BF),
            pltpu.VMEM(big, BF),
            pltpu.VMEM(big, BF),
            pltpu.VMEM((SPARE + 1, 8, 2 * R), F32),
            pltpu.VMEM((SPARE + 1, 8, 2 * R), F32),
            pltpu.VMEM((F, R), F32),
            pltpu.VMEM((WIN, F), F32),
            pltpu.VMEM((WIN, 128), F32),
            pltpu.VMEM((WIN, 128), F32),
            pltpu.VMEM((WIN, 128), F32),
            pltpu.VMEM((F, F), F32),
            pltpu.VMEM((48, 128), F32),
            pltpu.VMEM((F, R), F32),
            pltpu.SemaphoreType.DMA((OWN,)),
        ]
        + [pltpu.VMEM(big[1:], BF)] * (4 * STEP)
        + [pltpu.VMEM((8, 2 * R), F32)] * STEP
        + [pltpu.VMEM((F, 128), F32)] * STEP,
        compiler_params=pltpu.CompilerParams(vmem_limit_bytes=60 * 2**20),
        interpret=interpret,
    )(dev, counts, reads, starts, x, conv_w, bias, mix, query, cot)


def on_device(
    read_blocks, block_counts, block_reads, block_starts,
    conv_weight, conv_bias, mix_weight, pool_query, site_cotangent,
):
    dev = lax.axis_index(SAMP).astype(jnp.int32).reshape(1)
    pooled, grads = run_kernel(
        dev, block_counts, block_reads, block_starts,
        read_blocks,
        conv_weight.reshape(3 * CH, F), conv_bias.reshape(1, F), mix_weight,
        pool_query.reshape(1, F), site_cotangent[0, 0],
    )
    grads = jnp.sum(lax.all_to_all(grads, ("x", "core"), 0, 0), axis=0)
    for axes in (("z_low", "rep"), "z_high"):
        every = jnp.broadcast_to(grads, (8, *grads.shape))
        grads = jnp.sum(lax.all_to_all(every, axes, 0, 0), axis=0)
    g_mix = jnp.concatenate([grads[:32, :F], grads[:32, F:]], axis=0)
    rest = jnp.concatenate([grads[32:, :F], grads[32:, F:]], axis=0)
    return (pooled[None, None], rest[:24].reshape(3, CH, F), rest[24], g_mix, rest[25])


def solution(mesh):
    split = jax.sharding.Mesh(
        mesh.devices.reshape(8, 2, 4, 2, mesh.shape["rep"]), SAMP + ("rep",)
    )
    in_specs = (
        P("rep", SAMP, None, None, None),
        P("rep", None),
        P("rep", None),
        P("rep", None),
        P(),
        P(),
        P(),
        P(),
        P("rep", SAMP, None, None),
    )
    out_specs = (P("rep", SAMP, None, None), P(), P(), P(), P())
    return jax.shard_map(
        on_device, mesh=split, in_specs=in_specs, out_specs=out_specs, check_vma=False
    )
```

```python
import jax
import jax.numpy as jnp
from jax import lax
from jax.experimental import pallas as pl
from jax.experimental.pallas import tpu as pltpu
from jax.sharding import PartitionSpec as P

POS = 221
CH = 8
R = 128
F = 64
OWN = 4
SITES = 1024
HALF = 112
GROUP = 8
CHUNKS = HALF // GROUP
XPOS = 2 * HALF + 2
WIN = SITES + 8
SPARE = OWN * CHUNKS
STEP = 4

SAMP = ("z_high", "z_low", "x", "core")

F32 = jnp.float32
BF = jnp.bfloat16
NT = (((1,), (1,)), ((), ()))


def mm(a, b):
    return jnp.dot(a, b, preferred_element_type=F32)


def mm_nt(a, b):
    return lax.dot_general(a, b, NT, preferred_element_type=F32)


def split2(v):
    hi = v.astype(BF)
    return hi, (v - hi.astype(F32)).astype(BF)


def spread(v):
    twice = jnp.concatenate([v, v], axis=1)
    row = lax.broadcasted_iota(jnp.int32, twice.shape, 0) % GROUP
    late = lax.broadcasted_iota(jnp.int32, twice.shape, 1) // F
    return jnp.concatenate(
        [jnp.where(row == 2 * m + late, twice, 0.0) for m in range(GROUP // 2)], axis=1
    )


def halves(v):
    zero = jnp.zeros((8, R), v.dtype)
    left = jnp.concatenate([v[:, :R], zero], axis=1)
    right = jnp.concatenate([zero, v[:, R:]], axis=1)
    return jnp.concatenate([left, right], axis=0)


def pooling_kernel(
    dev, counts, reads, starts, x_hbm, conv_w, bias, mix, query, cot_hbm,
    pooled_hbm, grads,
    x, hid, feat, slope, weight_rows, gate_rows, query_rows,
    w_num, w_den, d_num, d_den, acc_mix, acc_conv, acc_query, cot, pooled, sems, *rings,
):
    me = dev[0]
    count = counts[0, me]
    total = count * CHUNKS
    hid_ring, feat_ring, second_ring, relu_ring, score_ring, turned_ring = (
        rings[STEP * n : STEP * n + STEP] for n in range(6)
    )

    copies = [
        pltpu.make_async_copy(x_hbm.at[0, s], x.at[s, pl.ds(1, POS)], sems.at[s])
        for s in range(OWN)
    ]
    cot_copy = pltpu.make_async_copy(cot_hbm, cot, sems.at[OWN])
    pooled_copy = pltpu.make_async_copy(pooled, pooled_hbm, sems.at[OWN + 1])
    for copy in copies:
        copy.start()
    cot_copy.start()
    for s in range(OWN):
        x[s, 0] = jnp.zeros((CH, R), BF)
        x[s, POS + 1 :] = jnp.zeros((XPOS - POS - 1, CH, R), BF)

    zeros = lambda *s: jnp.zeros(s, F32)
    cw = conv_w[...].astype(F32)
    b = bias[...]
    b_hi = b.astype(BF).astype(F32)
    b_mid = (b - b_hi).astype(BF).astype(F32)
    b_lo = b - b_hi - b_mid
    b_rows = jnp.concatenate([b_hi, b_mid, b_lo, zeros(13, F)], axis=0)
    even = jnp.concatenate([cw, zeros(8, F), b_rows, zeros(80, F)], axis=0)
    odd = jnp.concatenate([zeros(8, F), cw, b_rows, zeros(80, F)], axis=0)
    conv_lhs = jnp.concatenate([even.T, odd.T], axis=0)[:, :48].astype(BF)
    pad_mix = jnp.concatenate([mix[...].astype(F32), zeros(64, F)], axis=0)
    mix_t = (0.5 * pad_mix.T[:, :F]).astype(BF)
    mix_b = mix[...]
    q = 0.5 * query[...]
    q_hi = q.astype(BF).astype(F32)
    q_lo = q - q_hi
    query_lhs = spread(
        jnp.concatenate([jnp.broadcast_to(q_hi, (8, F)), jnp.broadcast_to(q_lo, (8, F))], axis=0)
    ).astype(BF)
    query_rows[...] = jnp.concatenate([jnp.broadcast_to(q, (128, F)), zeros(128, F)], axis=1).T[:F]
    ones = jnp.ones((16, 2 * R), BF)
    row8 = lax.broadcasted_iota(jnp.int32, (8, 2 * R), 0)
    lane8 = lax.broadcasted_iota(jnp.int32, (8, 2 * R), 1)
    row16 = lax.broadcasted_iota(jnp.int32, (16, 128), 0) % GROUP
    pair16 = row16 // 2

    def place(k):
        slot = jnp.int32(0)
        for s in range(1, OWN):
            slot = slot + (k >= s * CHUNKS).astype(jnp.int32)
        return slot, k - slot * CHUNKS

    def window(slot, c, i):
        at = c * GROUP + 2 * i
        left = x[slot, pl.ds(at, 4)].reshape(32, R)
        right = x[slot, pl.ds(at + HALF, 4)].reshape(32, R)
        return jnp.concatenate([jnp.concatenate([left, right], axis=1), ones], axis=0)

    w_num[...] = jnp.zeros(w_num.shape, F32)
    w_den[...] = jnp.zeros(w_den.shape, F32)
    copies[0].wait()

    def first_dots(k, half, i):
        slot, c = place(jnp.minimum(k, SPARE - 1))
        pre = mm(conv_lhs, window(slot, c, i)).astype(BF)
        rows = slice(128 * i, 128 * i + 128)
        relu = jnp.maximum(pre, jnp.zeros_like(pre))
        hid[k, rows, :] = relu
        hid_ring[half][rows, :] = relu

    def second_dot(half, j):
        return mm(mix_t, hid_ring[half][F * j : F * j + F, :])

    def score_dot(half, n):
        rows = slice(128 * n, 128 * n + 128)
        return mm(query_lhs[:, rows], feat_ring[half][rows, :])

    def second_rest(k, dots):
        for j, h in enumerate(dots):
            rows = slice(F * j, F * j + F)
            t = jnp.tanh(h)
            a = 1.0 + t
            f = h * a
            feat[k, rows, :] = f.astype(BF)
            slope[k, rows, :] = (a + f * (1.0 - t)).astype(BF)

    def score_stage(k, score):
        slot, c = place(k)
        score = score[:8] + score[8:]
        opening = 0.5 + 0.5 * jnp.tanh(score)
        read = jnp.where(lane8 < R, lane8, lane8 - R)
        position = jnp.where(lane8 < R, row8, row8 + HALF) + GROUP * c
        live = (read < reads[0, me * OWN + slot]) & (position < POS)
        weight = jnp.where(live, opening, 0.0)
        weight_rows[k] = weight
        gate_rows[k] = weight * (1.0 - opening)
        dens = [
            jnp.broadcast_to(jnp.sum(weight[:, at : at + R], axis=1, keepdims=True), (8, 128))
            for at in (0, R)
        ]
        return halves(weight).astype(BF), dens

    def pool_dot(half, lhs, num, n):
        part = mm_nt(lhs, feat_ring[half][256 * n : 256 * n + 256, :])
        for m in range(2):
            num = jnp.where(pair16 == 2 * n + m, part[:, 128 * m : 128 * m + 128], num)
        return num

    def pool_rest(k, dens, num, valid):
        slot, c = place(k)
        first = starts[0, me * OWN + slot] + GROUP * c
        num = jnp.where(row16 % 2 == 0, num, pltpu.roll(num, F, 1))[:, :F]
        for part, den, at in ((num[:8], dens[0], first), (num[8:], dens[1], first + HALF)):
            here = pl.ds(at, 8)
            w_num[here, :] += jnp.where(valid, part, 0.0)
            w_den[here, :] += jnp.where(valid, den, 0.0)

    inside = lambda v: (v >= 0) & (v < total)
    bound = lambda v: jnp.clip(v, 0, SPARE - 1)
    steps = (total + STEP - 1) // STEP

    def forward_step(i, stages):
        first, second, pool = (n in stages for n in range(3))
        chunks = range(STEP)
        new = [jnp.minimum(STEP * i + n, SPARE) for n in chunks]
        mid = [jnp.clip(STEP * (i - 1) + n, 0, SPARE) for n in chunks]
        old = [bound(STEP * (i - 2) + n) for n in chunks]
        nums = [jnp.zeros((16, 128), F32)] * STEP
        scores = [jnp.zeros((16, 2 * R), F32)] * STEP
        weights, dots = {}, [[] for _ in chunks]

        def mix_chunk(n, scored=()):
            for j in range(GROUP):
                if second:
                    dots[n].append(second_dot(n, j))
                if pool and j % 2:
                    for p in scored:
                        scores[p] += score_dot(p, j // 2)
            if pool:
                for p in scored:
                    weights[p] = score_stage(old[p], scores[p])
            if second:
                second_rest(mid[n], dots[n])

        def convolve_chunk(n, pooled=()):
            for m in range(GROUP // 2):
                if first:
                    first_dots(new[n], n, m)
                if pool:
                    for p in pooled[m // 2 : m // 2 + 1]:
                        nums[p] = pool_dot(p, weights[p][0], nums[p], m % 2)
            if pool:
                for p in pooled:
                    pool_rest(old[p], weights[p][1], nums[p], inside(STEP * (i - 2) + p))

        mix_chunk(0, (0, 1))
        mix_chunk(1, (2, 3))
        convolve_chunk(0, (0, 1))
        mix_chunk(2)
        convolve_chunk(1, (2, 3))
        mix_chunk(3)
        convolve_chunk(2)
        convolve_chunk(3)
        if second:
            for n in chunks:
                feat_ring[n][...] = feat[mid[n]]

    forward_step(0, (0,))
    forward_step(1, (0, 1))
    for copy in copies[1:]:
        copy.wait()

    @pl.loop(2, steps)
    def _(i):
        forward_step(i, (0, 1, 2))

    forward_step(steps, (1, 2))
    forward_step(steps + 1, (2,))

    cot_copy.wait()
    d_num[SITES:, :] = jnp.zeros((WIN - SITES, 128), F32)
    d_den[SITES:, :] = jnp.zeros((WIN - SITES, 128), F32)
    for i in range(SITES // 128):
        here = slice(128 * i, 128 * i + 128)
        num = w_num[here, :]
        den = w_den[here, :]
        inv = 1.0 / jnp.maximum(den, 1.0)
        out = jnp.concatenate([num * inv[:, :F], jnp.zeros((128, F), F32)], axis=1)
        pooled[:, here] = out.T[:F]
        cot_t = jnp.concatenate([cot[:, here], jnp.zeros((F, 128), F32)], axis=0).T
        dn = cot_t * inv
        d_num[here, :] = dn
        inner = jnp.sum(dn[:, :F] * num, axis=1, keepdims=True)
        d_den[here, :] = jnp.where(den > 1.0, -(jnp.broadcast_to(inner, (128, 128)) * inv), 0.0)

    pooled_copy.start()

    acc_mix[...] = jnp.zeros(acc_mix.shape, F32)
    acc_conv[...] = jnp.zeros(acc_conv.shape, F32)
    acc_query[...] = jnp.zeros(acc_query.shape, F32)

    def cut(k):
        slot, c = place(k)
        first = starts[0, me * OWN + slot] + GROUP * c
        return first, jnp.concatenate(
            [d_num[pl.ds(first, 8), :], d_num[pl.ds(first + HALF, 8), :]], axis=0
        )

    def second_back(k, half, valid):
        turned = turned_ring[half][...]
        q = query_rows[...]
        sums = zeros(F, R)
        for j in range(GROUP):
            rows = slice(F * j, F * j + F)
            f = feat[k, rows, :].astype(F32)
            e = slope[k, rows, :].astype(F32)
            out = []
            for side in range(2):
                lanes = slice(R * side, R * side + R)
                at = GROUP * side + j
                w = weight_rows[k, j : j + 1, lanes]
                s = score_ring[half][j : j + 1, lanes]
                d_feat = turned[:, at : at + 1] * w + q * s
                out.append((d_feat * e[:, lanes]).astype(BF))
                sums = sums + f[:, lanes] * s
            second_ring[half][rows, :] = jnp.concatenate(out, axis=1)
        acc_query[...] += jnp.where(valid, sums, 0.0)

    def backward_step(i, stages):
        weight, second, relu, conv = (n in stages for n in range(4))
        for half in range(STEP):
            k0, k1, k2, k3 = (STEP * (i - lag) + half for lag in range(4))
            new, old, last = bound(k0), bound(k2), bound(k3)
            slot, c = place(last)
            g_conv = zeros(48, 128)
            g_mix = zeros(F, F)
            for n in range(GROUP // 2):
                both = slice(128 * n, 128 * n + 128)
                if conv:
                    g_conv += mm_nt(window(slot, c, n), relu_ring[half][both, :])
                if relu:
                    h = [hid[old, F * j : F * j + F, :] for j in (2 * n, 2 * n + 1)]
                    d2 = [second_ring[half][F * j : F * j + F, :] for j in (2 * n, 2 * n + 1)]
                    for j in range(2):
                        dh = mm(mix_b, d2[j]).astype(BF)
                        at = F * (2 * n + j)
                        relu_ring[half][at : at + F, :] = jnp.where(
                            h[j] > 0, dh, jnp.zeros_like(dh)
                        )
                    g_mix += mm_nt(jnp.concatenate(h, axis=1), jnp.concatenate(d2, axis=1))
            if second:
                second_back(bound(k1), half, inside(k1))
            if weight:
                first, dn = cut(new)
                hi, lo = split2(spread(dn[:, :F]))
                dw = mm(jnp.concatenate([hi, lo], axis=0), feat[new])
                dw = jnp.concatenate(
                    [dw[:8, :R] + dw[16:24, :R], dw[8:16, R:] + dw[24:, R:]], axis=1
                )
                dd = jnp.concatenate(
                    [d_den[pl.ds(first, 8), :], d_den[pl.ds(first + HALF, 8), :]], axis=1
                )
                score_ring[half][...] = (dw + dd) * gate_rows[new]
                turned_ring[half][...] = jnp.concatenate([0.5 * dn, zeros(112, 128)], axis=0).T[:F]
            if conv:
                acc_conv[...] += jnp.where(inside(k3), g_conv, 0.0)
            if relu:
                acc_mix[...] += jnp.where(inside(k2), g_mix, 0.0)

    backward_step(0, (0,))
    backward_step(1, (0, 1))
    backward_step(2, (0, 1, 2))

    @pl.loop(3, steps)
    def _(i):
        backward_step(i, (0, 1, 2, 3))

    backward_step(steps, (1, 2, 3))
    backward_step(steps + 1, (2, 3))
    backward_step(steps + 2, (3,))

    turned = acc_conv[...]
    g_conv = turned[0:24, :F] + turned[8:32, F:]
    g_bias = turned[32:33, :F] + turned[32:33, F:]
    ones_f = jnp.concatenate([acc_query[...], zeros(F, R)], axis=0).T
    g_query = jnp.sum(ones_f, axis=0, keepdims=True)[:, :F]
    rest = jnp.concatenate([g_conv, g_bias, g_query, zeros(6, F)], axis=0)
    gm = acc_mix[...]
    packed = jnp.concatenate(
        [jnp.concatenate([v[:n], v[n:]], axis=1) for v, n in ((gm, 32), (rest, 16))], axis=0
    )
    for n in range(GROUP):
        grads[n] = packed
    pooled_copy.wait()


def finish_kernel(parts, g_conv, g_bias, g_mix, g_query):
    total = parts[0]
    for n in range(1, GROUP):
        total += parts[n]
    left, right = total[:, :F], total[:, F:]
    g_mix[:32, :] = left[:32]
    g_mix[32:, :] = right[:32]
    g_conv[:16, :] = left[32:]
    g_conv[16:, :] = right[32:40]
    g_bias[...] = right[40:41]
    g_query[...] = right[41:42]


def run_kernel(dev, counts, reads, starts, x, conv_w, bias, mix, query, cot, interpret=False):
    smem = pl.BlockSpec(memory_space=pltpu.SMEM)
    vmem = pl.BlockSpec(memory_space=pltpu.VMEM)
    anywhere = pl.BlockSpec(memory_space=pl.ANY)
    big = (SPARE + 1, GROUP * F, 2 * R)
    return pl.pallas_call(
        pooling_kernel,
        out_shape=(
            jax.ShapeDtypeStruct((F, SITES), F32),
            jax.ShapeDtypeStruct((GROUP, 48, 128), F32),
        ),
        in_specs=[smem] * 4 + [anywhere] + [vmem] * 4 + [anywhere],
        out_specs=(anywhere, vmem),
        scratch_shapes=[
            pltpu.VMEM((OWN, XPOS, CH, R), BF),
            pltpu.VMEM(big, BF),
            pltpu.VMEM(big, BF),
            pltpu.VMEM(big, BF),
            pltpu.VMEM((SPARE + 1, 8, 2 * R), F32),
            pltpu.VMEM((SPARE + 1, 8, 2 * R), F32),
            pltpu.VMEM((F, R), F32),
            pltpu.VMEM((WIN, F), F32),
            pltpu.VMEM((WIN, 128), F32),
            pltpu.VMEM((WIN, 128), F32),
            pltpu.VMEM((WIN, 128), F32),
            pltpu.VMEM((F, F), F32),
            pltpu.VMEM((48, 128), F32),
            pltpu.VMEM((F, R), F32),
            pltpu.VMEM((F, SITES), F32),
            pltpu.VMEM((F, SITES), F32),
            pltpu.SemaphoreType.DMA((OWN + 2,)),
        ]
        + [pltpu.VMEM(big[1:], BF)] * (4 * STEP)
        + [pltpu.VMEM((8, 2 * R), F32)] * STEP
        + [pltpu.VMEM((F, 128), F32)] * STEP,
        compiler_params=pltpu.CompilerParams(vmem_limit_bytes=60 * 2**20),
        interpret=interpret,
    )(dev, counts, reads, starts, x, conv_w, bias, mix, query, cot)


def on_device(
    read_blocks, block_counts, block_reads, block_starts,
    conv_weight, conv_bias, mix_weight, pool_query, site_cotangent,
):
    dev = lax.axis_index(SAMP).astype(jnp.int32).reshape(1)
    pooled, grads = run_kernel(
        dev, block_counts, block_reads, block_starts,
        read_blocks,
        conv_weight.reshape(3 * CH, F), conv_bias.reshape(1, F), mix_weight,
        pool_query.reshape(1, F), site_cotangent[0, 0],
    )
    parts = lax.all_to_all(grads, ("x", "core"), 0, 0)
    for axes in (("z_low", "rep"), "z_high"):
        total = jnp.sum(parts, axis=0)
        parts = lax.all_to_all(jnp.broadcast_to(total, parts.shape), axes, 0, 0)
    vmem = pl.BlockSpec(memory_space=pltpu.VMEM)
    shapes = [(3 * CH, F), (1, F), (F, F), (1, F)]
    g_conv, g_bias, g_mix, g_query = pl.pallas_call(
        finish_kernel,
        out_shape=[jax.ShapeDtypeStruct(shape, F32) for shape in shapes],
        in_specs=[vmem],
        out_specs=[vmem] * 4,
    )(parts)
    return (
        pooled[None, None], g_conv.reshape(3, CH, F), g_bias.reshape(F), g_mix, g_query.reshape(F)
    )


def solution(mesh):
    split = jax.sharding.Mesh(
        mesh.devices.reshape(8, 2, 4, 2, mesh.shape["rep"]), SAMP + ("rep",)
    )
    in_specs = (
        P("rep", SAMP, None, None, None),
        P("rep", None),
        P("rep", None),
        P("rep", None),
        P(),
        P(),
        P(),
        P(),
        P("rep", SAMP, None, None),
    )
    out_specs = (P("rep", SAMP, None, None), P(), P(), P(), P())
    return jax.shard_map(
        on_device, mesh=split, in_specs=in_specs, out_specs=out_specs, check_vma=False
    )
```
